32 devices in a mesh: rep: 2 (over y), pool: 2 (over core), tp: 8 (over z, x).
Axes of the slice: x: 2, y: 2, z: 4, core: 2. Of those that a mesh axis runs over, the one named last changes fastest.
Arguments:
- hidden: bfloat16 [512, 16384], P(('rep', 'pool'), 'tp'), parts along dimension 0, may hold values from -6 to 6
- row_request_slots: int32 [512], P('rep'), parts along dimension 0, may hold values from 0 to 31
- requests: int32 [4, 32], P('rep'), parts along dimension 0, may hold values from 0 to 127
- adapter_page_table: int32 [128], replicated, may hold values from 0 to 127, each once
- down_matrix: bfloat16 [16384, 8192], P('tp'), may hold values from -0.046875 to 0.046875
- shrink_pool_pages: bfloat16 [128, 64, 16384], P('pool', None, 'tp'), may hold values from -0.046875 to 0.046875
- expand_pool_pages: bfloat16 [128, 64, 8192], P('pool', None, 'tp'), may hold values from -0.75 to 0.75
Outputs:
- projected: bfloat16 [512, 8192], P(('rep', 'pool'), 'tp'), parts along dimension 0
The draws below stay inside these ranges and needn't reach their ends.
There are 2 independent parts, one for each index of `rep`. The reference program is written for one: setup_inputs(seed, part) draws one part's arguments, and reference() takes and returns one part's arrays. A program takes and returns all parts, laid end to end along the dimension named above; an argument that names none is the same for every part. Nothing has to cross between parts.
All inputs are finite; a program needn't handle non-finite values.
Results may differ from the reference program's by a relative error of at most 0.0039.
Values may be sent and summed in bfloat16 or wider, within the bound.
A program may use at most 256 MiB of HBM per device.

```python
import math
import jax
import jax.numpy as jnp
import numpy as np
from jax import lax

MODEL_WIDTH = 8192
HIDDEN_UNITS = 16384
ADAPTER_RANK = 64
R_DEV = 128
MAXREQ = 32
ROWS = 256
ADAPTER_COUNT = 128
N_POOL = 2


def set_ends(entries, stream_key, smallest, high):
    longest = entries.shape.index(max(entries.shape))
    spots = []
    for shift in (0, 1):
        where = [jax.random.randint(jax.random.fold_in(stream_key, axis), (), 0, length) for axis, length in enumerate(entries.shape)]
        where[longest] = (where[longest] + shift) % entries.shape[longest]
        spots.append(tuple(where))
    return entries.at[spots[0]].set(smallest).at[spots[1]].set(high)


def shard_levels(key, dims, cuts, low, high):
    loudness = 1.0
    for axis_at, shards_of in cuts:
        steps = jax.random.uniform(jax.random.fold_in(jax.random.fold_in(key, 6), axis_at), (shards_of,), jnp.float32, low / len(cuts), high / len(cuts))
        loudness = loudness * jnp.repeat(jnp.exp(steps), dims[axis_at] // shards_of).reshape((-1,) + (1,) * (len(dims) - 1 - axis_at))
    return loudness


def rank_bounds(amount, skew):
    loads = [(1 << 20) // math.isqrt(standing ** skew) + 1 for standing in range(1, amount + 1)]
    spread = 1 + sum(loads) // (1 << 30)
    return np.cumsum(np.array([max(1, weight // spread) for weight in loads]))


def ranked(own_key, shape, number_of, slope):
    grid = rank_bounds(number_of, slope)
    lot = jax.random.randint(jax.random.fold_in(own_key, 1), shape, 0, int(grid[number_of - 1]))
    standing = jnp.searchsorted(jnp.asarray(grid, jnp.int32), lot, side="right")
    return jax.random.permutation(jax.random.fold_in(own_key, 2), number_of)[standing].astype(jnp.int32)


def centred(key, shape, scale, bound, split=(), kind=jnp.bfloat16):
    result = jax.random.normal(key, shape, jnp.float32) * scale
    if len(split) > 0:
        result = shard_levels(key, shape, split, -0.22, 0.18) * result
    return jnp.clip(result, min=-bound, max=bound).astype(kind)


def setup_inputs(seed: int = 0, part: int = 0) -> dict:
    arg_keys = jax.random.split(jax.random.key(seed), 8)
    part_splits = jax.random.split(jax.random.fold_in(arg_keys[7], part), 8)
    hidden = centred(part_splits[0], (ROWS, HIDDEN_UNITS), 1.0, 6.0, ((0, 2), (1, 8)))
    row_request_slots = set_ends(ranked(part_splits[1], (ROWS,), MAXREQ, 2), jax.random.fold_in(part_splits[1], 3), 0, MAXREQ - 1).astype(jnp.int32)
    requests = set_ends(jax.random.randint(part_splits[2], (N_POOL, MAXREQ), 0, ADAPTER_COUNT), jax.random.fold_in(part_splits[2], 1), 0, ADAPTER_COUNT - 1).astype(jnp.int32)
    adapter_page_table = jax.random.permutation(arg_keys[3], ADAPTER_COUNT).astype(jnp.int32)
    down_matrix = centred(arg_keys[4], (HIDDEN_UNITS, MODEL_WIDTH), HIDDEN_UNITS ** -0.5, 0.046875, ((0, 8),))
    shrink_pool_pages = centred(arg_keys[5], (ADAPTER_COUNT, ADAPTER_RANK, HIDDEN_UNITS), HIDDEN_UNITS ** -0.5, 0.046875, ((0, 2), (2, 8)))
    expand_pool_pages = centred(arg_keys[6], (ADAPTER_COUNT, ADAPTER_RANK, MODEL_WIDTH), ADAPTER_RANK ** -0.5, 0.75, ((0, 2), (2, 8)))
    return dict(hidden=hidden, row_request_slots=row_request_slots, requests=requests, adapter_page_table=adapter_page_table, down_matrix=down_matrix, shrink_pool_pages=shrink_pool_pages, expand_pool_pages=expand_pool_pages)


def reference(hidden, row_request_slots, requests, adapter_page_table, down_matrix, shrink_pool_pages, expand_pool_pages):
    base_output = jnp.dot(hidden, down_matrix, preferred_element_type=jnp.float32)
    row_groups = (jnp.arange(ROWS, dtype=jnp.int32) // R_DEV).astype(jnp.int32)
    adapters = requests[row_groups, row_request_slots]
    page_numbers = jnp.take(adapter_page_table, adapters, axis=0).astype(jnp.int32)

    def single_row(packed):
        row_hidden_input, page_number = packed
        rank_activation = jnp.dot(shrink_pool_pages[page_number], row_hidden_input, preferred_element_type=jnp.float32).astype(jnp.bfloat16)
        return jnp.dot(rank_activation, expand_pool_pages[page_number], preferred_element_type=jnp.float32)

    adapter_update = lax.map(single_row, (hidden, page_numbers))
    return (base_output + adapter_update).astype(jnp.bfloat16)
```

```python
import functools

import jax
import jax.numpy as jnp
from jax import lax
from jax.experimental import pallas as pl
from jax.experimental.pallas import tpu as pltpu
from jax.sharding import PartitionSpec as P

MESH = pl.DeviceIdType.MESH
DEPTH = 6


def owner_split(adapters, adapter_page_table, per_holder_count):
    page_numbers = jnp.take(adapter_page_table, adapters, axis=0)
    return (page_numbers // per_holder_count, page_numbers % per_holder_count)


def shrink_select(rows_in, pages_a, onehot_picker):
    scores = jnp.einsum("rf,pkf->rpk", rows_in, pages_a, preferred_element_type=jnp.float32)
    return jnp.sum(scores * onehot_picker[:, :, None], axis=1)


def expand_choice_mask(rank_activation, expand_page_rows, onehot_picker):
    weighted = (onehot_picker[:, :, None] * rank_activation.astype(jnp.float32)[:, None, :]).astype(
        jnp.bfloat16
    )
    flat_rows = weighted.reshape(weighted.shape[0], -1)
    flat_pages = expand_page_rows.reshape(-1, expand_page_rows.shape[2])
    return jnp.dot(flat_rows, flat_pages, preferred_element_type=jnp.float32)


def local_general(
    hidden,
    row_request_slots,
    requests,
    adapter_page_table,
    down_matrix,
    shrink_pool_pages,
    expand_pool_pages,
):
    rows_dev = hidden.shape[0]
    per_holder_count = shrink_pool_pages.shape[0]
    pool_index = lax.axis_index("pool")
    partial_value = jnp.dot(hidden, down_matrix, preferred_element_type=jnp.float32)
    base_output = lax.psum_scatter(partial_value, "tp", scatter_dimension=1, tiled=True)
    owner_index, shard_local_pages = owner_split(requests, adapter_page_table, per_holder_count)
    holder_slots = (owner_index == pool_index)[:, :, None, None]
    empty_filler = jnp.zeros((), jnp.bfloat16)
    sent_shrink_pages = jnp.where(
        holder_slots, jnp.take(shrink_pool_pages, shard_local_pages, axis=0), empty_filler
    )
    sent_expand_pages = jnp.where(
        holder_slots, jnp.take(expand_pool_pages, shard_local_pages, axis=0), empty_filler
    )
    fetched_a, fetched_b = (
        lax.all_to_all(sent_shrink_pages, "pool", split_axis=0, concat_axis=0, tiled=True),
        lax.all_to_all(sent_expand_pages, "pool", split_axis=0, concat_axis=0, tiled=True),
    )
    pages_a = jnp.sum(fetched_a, axis=0)
    expand_page_rows = jnp.sum(fetched_b, axis=0)
    own_slots = lax.dynamic_slice_in_dim(row_request_slots, pool_index * rows_dev, rows_dev, 0)
    slot_range = jnp.arange(pages_a.shape[0], dtype=jnp.int32)
    onehot_picker = (own_slots[:, None] == slot_range[None, :]).astype(jnp.float32)
    shrink_part = shrink_select(hidden, pages_a, onehot_picker)
    rank_activation = lax.psum(shrink_part, "tp").astype(jnp.bfloat16)
    adapter_update = expand_choice_mask(rank_activation, expand_page_rows, onehot_picker)
    return (base_output + adapter_update).astype(jnp.bfloat16)


def fused_kernel(
    slots_ref,
    requests_ref,
    table_ref,
    hidden_ref,
    down_ref,
    shrink_ref,
    expand_ref,
    out_ref,
    hid,
    wbuf,
    sbuf,
    ebuf,
    own,
    xs,
    xr,
    zs,
    zr,
    bs,
    br,
    delta,
    ds_,
    dr,
    pack,
    lrr,
    lrs,
    lrg,
    load_sem,
    hid_sem,
    x_sem,
    z_sem,
    b_sem,
    d_sem,
    l_sem,
    g_sem,
):
    rep = lax.axis_index("rep")
    c = lax.axis_index("pool")
    tp = lax.axis_index("tp")
    z, x = tp // 2, tp % 2
    rows = hidden_ref.shape[0]
    half = out_ref.shape[1] // 2
    lane = lambda shape: lax.broadcasted_iota(jnp.int32, shape, 1)

    def dev(pool, t):
        return (rep, pool, t)

    zdest = [(z + 2) % 4, 3 - z, z + 1 - 2 * (z % 2), z]

    def column(zz, xx):
        return pl.multiple_of((zz * 2 + xx) * (2 * half) + c * half, half)

    def down_load(slot, zz, xx):
        return down_ref.at[:, pl.ds(column(zz, xx), half)], wbuf.at[slot]

    loads = []
    keys = {}

    def add(key, pair):
        k = len(loads)
        keys[key] = k
        loads.append(pltpu.make_async_copy(pair[0], pair[1], load_sem.at[k]))

    for i in (0, 1):
        add(("r", i), down_load(i, zdest[i], 1 - x))
    for i in (0, 1):
        add(("o", i), down_load(4 + i, zdest[i], x))
    for i in range(8):
        add(("s", i), (shrink_ref.at[pl.ds(i * 512, 512), :], sbuf.at[i]))
    for i in (2, 3):
        add(("r", i), down_load(i, zdest[i], 1 - x))
    for i in (2, 3):
        add(("o", i), down_load(4 + i, zdest[i], x))
    for i in range(4):
        add(("e", i), (expand_ref.at[pl.ds(i * 1024, 1024), :], ebuf.at[i]))

    mine = pl.ds(pl.multiple_of(c * rows, rows), rows)
    theirs = pl.ds(pl.multiple_of((1 - c) * rows, rows), rows)
    hid_local = pltpu.make_async_copy(hidden_ref, hid.at[mine], hid_sem.at[2])
    hid_local.start()
    for k in range(DEPTH):
        loads[k].start()

    def use(key):
        k = keys[key]
        loads[k].wait()
        if k + DEPTH < len(loads):
            loads[k + DEPTH].start()

    barrier = pltpu.get_barrier_semaphore()
    for step in range(1, 8):
        pl.semaphore_signal(barrier, inc=1, device_id=dev(c, (tp + step) % 8), device_id_type=MESH)
    for zz in zdest:
        pl.semaphore_signal(barrier, inc=1, device_id=dev(1 - c, zz * 2 + x), device_id_type=MESH)
    pl.semaphore_wait(barrier, 11)

    hid_swap = pltpu.make_async_remote_copy(
        src_ref=hidden_ref, dst_ref=hid.at[mine],
        send_sem=hid_sem.at[0], recv_sem=hid_sem.at[1],
        device_id=dev(1 - c, tp), device_id_type=MESH,
    )
    hid_swap.start()

    first_shard = lax.broadcasted_iota(jnp.int32, (2 * rows, 32), 0) < rows
    entry = jnp.where(first_shard, requests_ref[0:1, :], requests_ref[1:2, :])
    adapter = jnp.sum(
        jnp.where(lane((2 * rows, 32)) == slots_ref[...], entry, 0), axis=1, keepdims=True
    )
    page = jnp.sum(
        jnp.where(lane((2 * rows, 128)) == adapter, table_ref[...], 0), axis=1, keepdims=True
    )
    pid = page - c * 64
    pid2 = jnp.broadcast_to(pid, (2 * rows, 128)) - lane((2 * rows, 128)) // 64

    hid_local.wait()
    hid_swap.wait()

    xn = z * 2 + 1 - x
    x_copies = {}

    def remote_piece(i):
        use(("r", i))
        xs[i] = jnp.dot(hid[...], wbuf[i], preferred_element_type=jnp.float32).astype(jnp.bfloat16)
        for h in range(2):
            part = pl.ds(h * rows, rows)
            x_copies[i, h] = pltpu.make_async_remote_copy(
                src_ref=xs.at[i, part], dst_ref=xr.at[i, part],
                send_sem=x_sem.at[0, 2 * i + h], recv_sem=x_sem.at[1, 2 * i + h],
                device_id=dev(c, xn), device_id_type=MESH,
            )
            x_copies[i, h].start()

    def own_piece(i):
        use(("o", i))
        own[i] = jnp.dot(hid[...], wbuf[4 + i], preferred_element_type=jnp.float32)

    z_sends = []

    def forward(i):
        for h in range(2):
            x_copies[i, h].wait_recv()
            part = pl.ds(h * rows, rows)
            zs[i, part] = (own[i, part] + xr[i, part].astype(jnp.float32)).astype(jnp.bfloat16)
            copy = pltpu.make_async_remote_copy(
                src_ref=zs.at[i, part], dst_ref=zr.at[i, c],
                send_sem=z_sem.at[0, i, h], recv_sem=z_sem.at[1, i, c],
                device_id=dev(h, zdest[i] * 2 + x), device_id_type=MESH,
            )
            copy.start()
            z_sends.append(copy)

    remote_piece(0)
    remote_piece(1)
    own_piece(0)
    own_piece(1)

    acc = jnp.zeros((2 * rows, 128), jnp.float32)
    for i in range(8):
        use(("s", i))
        scores = lax.dot_general(
            hid[...], sbuf[i], (((1,), (1,)), ((), ())), preferred_element_type=jnp.float32
        )
        for j in range(4):
            acc = acc + jnp.where(pid2 == 8 * i + 2 * j, scores[:, j * 128 : j * 128 + 128], 0.0)
    acc = acc + pltpu.roll(acc, 64, 1)
    low = lane((rows, 128)) < 64
    pack[...] = jnp.where(low, acc[:rows], acc[rows:])

    l_copies = []
    for step in range(1, 8):
        to = (tp + step) % 8
        copy = pltpu.make_async_remote_copy(
            src_ref=pack.at[pl.ds(pl.multiple_of(to * 16, 16), 16)], dst_ref=lrr.at[step - 1],
            send_sem=l_sem.at[0, step - 1], recv_sem=l_sem.at[1, step - 1],
            device_id=dev(c, to), device_id_type=MESH,
        )
        copy.start()
        l_copies.append(copy)

    forward(0)
    remote_piece(2)
    remote_piece(3)
    own_piece(2)
    own_piece(3)
    forward(1)

    block = pl.ds(pl.multiple_of(tp * 16, 16), 16)
    total = pack[block, :]
    for step in range(1, 8):
        l_copies[step - 1].wait_recv()
        total = total + lrr[step - 1]
    lrs[...] = total.astype(jnp.bfloat16)
    lrg[block, :] = lrs[...]
    g_copies = []
    for step in range(1, 8):
        to = (tp + step) % 8
        copy = pltpu.make_async_remote_copy(
            src_ref=lrs, dst_ref=lrg.at[block],
            send_sem=g_sem.at[0, step - 1], recv_sem=g_sem.at[1, step - 1],
            device_id=dev(c, to), device_id_type=MESH,
        )
        copy.start()
        g_copies.append(copy)

    forward(2)

    for step in range(1, 8):
        g_copies[step - 1].wait_recv()
    packed = lrg[...].astype(jnp.float32)
    turned = pltpu.roll(packed, 64, 1)
    rank2 = jnp.concatenate(
        [jnp.where(low, packed, turned), jnp.where(low, turned, packed)], axis=0
    )
    for i in range(4):
        use(("e", i))
        weighted = jnp.concatenate(
            [
                jnp.where(pid2 == 16 * i + 2 * j, rank2, 0.0).astype(jnp.bfloat16)
                for j in range(8)
            ],
            axis=1,
        )
        part = jnp.dot(weighted, ebuf[i], preferred_element_type=jnp.float32)
        if i == 0:
            delta[...] = part
        else:
            delta[...] += part
    ds_[...] = delta[theirs, :]
    d_copy = pltpu.make_async_remote_copy(
        src_ref=ds_, dst_ref=dr, send_sem=d_sem.at[0], recv_sem=d_sem.at[1],
        device_id=dev(1 - c, tp), device_id_type=MESH,
    )
    d_copy.start()

    for h in range(2):
        x_copies[3, h].wait_recv()
    bs[...] = own[3, theirs, :] + xr[3, theirs, :].astype(jnp.float32)
    b_copy = pltpu.make_async_remote_copy(
        src_ref=bs, dst_ref=br, send_sem=b_sem.at[0], recv_sem=b_sem.at[1],
        device_id=dev(1 - c, tp), device_id_type=MESH,
    )
    b_copy.start()
    own_cols = pl.ds(pl.multiple_of(c * half, half), half)
    other_cols = pl.ds(pl.multiple_of((1 - c) * half, half), half)
    base_own = own[3, mine, :] + xr[3, mine, :].astype(jnp.float32)
    d_copy.wait_recv()
    base_own = base_own + delta[mine, own_cols] + dr[:, own_cols]
    b_copy.wait_recv()
    base_other = br[...] + delta[mine, other_cols] + dr[:, other_cols]
    for i in range(3):
        for k in range(2):
            pltpu.make_async_remote_copy(
                src_ref=zr.at[i, k], dst_ref=zr.at[i, k],
                send_sem=z_sem.at[0, i, k], recv_sem=z_sem.at[1, i, k],
                device_id=dev(1 - c, tp), device_id_type=MESH,
            ).wait_recv()
        base_own = base_own + zr[i, c].astype(jnp.float32)
        base_other = base_other + zr[i, 1 - c].astype(jnp.float32)
    out_ref[:, own_cols] = base_own.astype(jnp.bfloat16)
    out_ref[:, other_cols] = base_other.astype(jnp.bfloat16)

    for copy in [*x_copies.values(), *z_sends, *l_copies, *g_copies, d_copy, b_copy]:
        copy.wait_send()


def local_fused(
    hidden,
    row_request_slots,
    requests,
    adapter_page_table,
    down_matrix,
    shrink_pool_pages,
    expand_pool_pages,
):
    rows, depth = hidden.shape
    pages, rank, width = expand_pool_pages.shape
    half = width // 2
    bf16, f32 = jnp.bfloat16, jnp.float32
    vmem = pl.BlockSpec(memory_space=pltpu.VMEM)
    hbm = pl.BlockSpec(memory_space=pl.ANY)
    V = pltpu.VMEM
    dma = pltpu.SemaphoreType.DMA
    flat = pages * rank
    return pl.pallas_call(
        fused_kernel,
        out_shape=jax.ShapeDtypeStruct((rows, width), bf16),
        in_specs=[vmem, vmem, vmem, hbm, hbm, hbm, hbm],
        out_specs=vmem,
        scratch_shapes=[
            V((2 * rows, depth), bf16),
            V((8, depth, half), bf16),
            V((8, flat // 8, depth), bf16),
            V((4, flat // 4, width), bf16),
            V((4, 2 * rows, half), f32),
            V((4, 2 * rows, half), bf16),
            V((4, 2 * rows, half), bf16),
            V((3, 2 * rows, half), bf16),
            V((3, 2, rows, half), bf16),
            V((rows, half), f32),
            V((rows, half), f32),
            V((2 * rows, width), f32),
            V((rows, width), f32),
            V((rows, width), f32),
            V((rows, 128), f32),
            V((7, 16, 128), f32),
            V((16, 128), bf16),
            V((rows, 128), bf16),
            dma((20,)),
            dma((3,)),
            dma((2, 8)),
            dma((2, 3, 2)),
            dma((2,)),
            dma((2,)),
            dma((2, 7)),
            dma((2, 7)),
        ],
        compiler_params=pltpu.CompilerParams(
            collective_id=0, has_side_effects=True, vmem_limit_bytes=60 * 1024 * 1024
        ),
    )(
        row_request_slots.reshape(-1, 1),
        requests,
        adapter_page_table.reshape(1, -1),
        hidden,
        down_matrix,
        shrink_pool_pages.reshape(flat, depth),
        expand_pool_pages.reshape(flat, width),
    )


def solution(mesh):
    return jax.shard_map(
        local_fused if mesh.shape["tp"] == 8 else local_general,
        mesh=mesh,
        in_specs=(
            P(("rep", "pool"), "tp"),
            P("rep"),
            P("rep", None),
            P(),
            P("tp", None),
            P("pool", None, "tp"),
            P("pool", None, "tp"),
        ),
        out_specs=P(("rep", "pool"), "tp"),
        check_vma=False,
    )
```

```python
import functools

import jax
import jax.numpy as jnp
from jax import lax
from jax.experimental import pallas as pl
from jax.experimental.pallas import tpu as pltpu
from jax.sharding import PartitionSpec as P

MESH = pl.DeviceIdType.MESH
DEPTH = 6
SPLIT = 3


def owner_split(adapters, adapter_page_table, per_holder_count):
    page_numbers = jnp.take(adapter_page_table, adapters, axis=0)
    return (page_numbers // per_holder_count, page_numbers % per_holder_count)


def shrink_select(rows_in, pages_a, onehot_picker):
    scores = jnp.einsum("rf,pkf->rpk", rows_in, pages_a, preferred_element_type=jnp.float32)
    return jnp.sum(scores * onehot_picker[:, :, None], axis=1)


def expand_choice_mask(rank_activation, expand_page_rows, onehot_picker):
    weighted = (onehot_picker[:, :, None] * rank_activation.astype(jnp.float32)[:, None, :]).astype(
        jnp.bfloat16
    )
    flat_rows = weighted.reshape(weighted.shape[0], -1)
    flat_pages = expand_page_rows.reshape(-1, expand_page_rows.shape[2])
    return jnp.dot(flat_rows, flat_pages, preferred_element_type=jnp.float32)


def local_general(
    hidden,
    row_request_slots,
    requests,
    adapter_page_table,
    down_matrix,
    shrink_pool_pages,
    expand_pool_pages,
):
    rows_dev = hidden.shape[0]
    per_holder_count = shrink_pool_pages.shape[0]
    pool_index = lax.axis_index("pool")
    partial_value = jnp.dot(hidden, down_matrix, preferred_element_type=jnp.float32)
    base_output = lax.psum_scatter(partial_value, "tp", scatter_dimension=1, tiled=True)
    owner_index, shard_local_pages = owner_split(requests, adapter_page_table, per_holder_count)
    holder_slots = (owner_index == pool_index)[:, :, None, None]
    empty_filler = jnp.zeros((), jnp.bfloat16)
    sent_shrink_pages = jnp.where(
        holder_slots, jnp.take(shrink_pool_pages, shard_local_pages, axis=0), empty_filler
    )
    sent_expand_pages = jnp.where(
        holder_slots, jnp.take(expand_pool_pages, shard_local_pages, axis=0), empty_filler
    )
    fetched_a, fetched_b = (
        lax.all_to_all(sent_shrink_pages, "pool", split_axis=0, concat_axis=0, tiled=True),
        lax.all_to_all(sent_expand_pages, "pool", split_axis=0, concat_axis=0, tiled=True),
    )
    pages_a = jnp.sum(fetched_a, axis=0)
    expand_page_rows = jnp.sum(fetched_b, axis=0)
    own_slots = lax.dynamic_slice_in_dim(row_request_slots, pool_index * rows_dev, rows_dev, 0)
    slot_range = jnp.arange(pages_a.shape[0], dtype=jnp.int32)
    onehot_picker = (own_slots[:, None] == slot_range[None, :]).astype(jnp.float32)
    shrink_part = shrink_select(hidden, pages_a, onehot_picker)
    rank_activation = lax.psum(shrink_part, "tp").astype(jnp.bfloat16)
    adapter_update = expand_choice_mask(rank_activation, expand_page_rows, onehot_picker)
    return (base_output + adapter_update).astype(jnp.bfloat16)


def fused_kernel(
    slots_ref,
    requests_ref,
    table_ref,
    hidden_ref,
    down_ref,
    shrink_ref,
    expand_ref,
    out_ref,
    hid,
    wbuf,
    sbuf,
    ebuf,
    own,
    xs,
    xr,
    zs,
    pair,
    last,
    bs,
    br,
    delta,
    ds_,
    dr,
    pack,
    lrr,
    lrs,
    lrg,
    load_sem,
    hid_sem,
    x_sem,
    z_sem,
    b_sem,
    d_sem,
    l_sem,
    g_sem,
):
    rep = lax.axis_index("rep")
    c = lax.axis_index("pool")
    tp = lax.axis_index("tp")
    z, x = tp // 2, tp % 2
    rows = hidden_ref.shape[0]
    half = out_ref.shape[1] // 2
    f32, bf16 = jnp.float32, jnp.bfloat16
    lane = lambda shape: lax.broadcasted_iota(jnp.int32, shape, 1)

    def dev(pool, t):
        return (rep, pool, t)

    near, far = z + 1 - 2 * (z % 2), (z + 2) % 4
    zdest = [3 - z, far, near, z]

    def column(zz, xx):
        return pl.multiple_of((zz * 2 + xx) * (2 * half) + c * half, half)

    loads = []
    keys = {}

    def add(key, source, target):
        k = len(loads)
        keys[key] = k
        loads.append(pltpu.make_async_copy(source, target, load_sem.at[k]))

    def add_down(key, slot, zz, xx):
        add(key, down_ref.at[:, pl.ds(column(zz, xx), half)], wbuf.at[slot])

    for i in range(4):
        add_down(("r", i), i, zdest[i], 1 - x)
    for i in (0, 1):
        add_down(("o", i), 4 + i, zdest[i], x)
    for i in range(8):
        add(("s", i), shrink_ref.at[pl.ds(i * 512, 512), :], sbuf.at[i])
    for i in (3, 2):
        add_down(("o", i), 4 + i, zdest[i], x)
    for i in range(4):
        add(("e", i), expand_ref.at[pl.ds(i * 1024, 1024), :], ebuf.at[i])

    mine = pl.ds(pl.multiple_of(c * rows, rows), rows)
    theirs = pl.ds(pl.multiple_of((1 - c) * rows, rows), rows)
    halves = (mine, theirs)
    hid_local = pltpu.make_async_copy(hidden_ref, hid.at[mine], hid_sem.at[2])
    hid_local.start()
    for k in range(DEPTH):
        loads[k].start()

    def use(key):
        k = keys[key]
        loads[k].wait()
        if k + DEPTH < len(loads):
            loads[k + DEPTH].start()

    barrier = pltpu.get_barrier_semaphore()
    for step in range(1, 8):
        pl.semaphore_signal(barrier, inc=1, device_id=dev(c, (tp + step) % 8), device_id_type=MESH)
    xn = z * 2 + 1 - x
    for t in (tp, xn, near * 2 + x, far * 2 + x):
        pl.semaphore_signal(barrier, inc=1, device_id=dev(1 - c, t), device_id_type=MESH)
    pl.semaphore_wait(barrier, 11)

    pending = []

    def send(src, dst, sems, index, pool, t):
        copy = pltpu.make_async_remote_copy(
            src_ref=src, dst_ref=dst,
            send_sem=sems.at[(0, *index)], recv_sem=sems.at[(1, *index)],
            device_id=dev(pool, t), device_id_type=MESH,
        )
        copy.start()
        pending.append(copy)
        return copy

    hid_swap = pltpu.make_async_remote_copy(
        src_ref=hidden_ref, dst_ref=hid.at[mine],
        send_sem=hid_sem.at[0], recv_sem=hid_sem.at[1],
        device_id=dev(1 - c, tp), device_id_type=MESH,
    )
    hid_swap.start()
    x_copies = {}

    def send_x(i, h):
        if i < 3:
            pool, target = c, xr.at[i, halves[h]]
        else:
            pool, target = (c, 1 - c)[h], last.at[0, h]
        x_copies[i, h] = send(xs.at[i, halves[h]], target, x_sem, (2 * i + h,), pool, xn)

    hid_local.wait()
    use(("r", 0))
    for h in range(2):
        if h == 1:
            hid_swap.wait()
        xs[0, halves[h]] = jnp.dot(
            hid[halves[h], :], wbuf[0], preferred_element_type=f32
        ).astype(bf16)
        send_x(0, h)
    for i in range(1, 4):
        use(("r", i))
        xs[i] = jnp.dot(hid[...], wbuf[i], preferred_element_type=f32).astype(bf16)
        for h in range(2):
            send_x(i, h)

    def own_piece(i):
        use(("o", i))
        own[i] = jnp.dot(hid[...], wbuf[4 + i], preferred_element_type=f32)

    z_copies = {}

    def forward(i):
        for h in range(2):
            part = halves[h]
            x_copies[i, h].wait_recv()
            total = own[i, part] + xr[i, part].astype(f32)
            if i == 1:
                z_copies[0, h].wait_recv()
                total = total + pair[part, :].astype(f32)
            zs[i, part] = total.astype(bf16)
            if i == 0:
                pool, target = c, pair.at[part]
            else:
                pool, target = (c, 1 - c)[h], last.at[i, h]
            z_copies[i, h] = send(
                zs.at[i, part], target, z_sem, (i, h), pool, (far if i == 1 else near) * 2 + x
            )

    own_piece(0)
    own_piece(1)

    pids = []
    for s in range(2):
        slot = jnp.transpose(jnp.broadcast_to(slots_ref[s : s + 1, :], (rows, rows)))
        adapter = jnp.sum(
            jnp.where(lane((rows, 32)) == slot[:, :32], requests_ref[s : s + 1, :], 0),
            axis=1, keepdims=True,
        )
        pids.append(
            jnp.sum(
                jnp.where(lane((rows, 128)) == adapter, table_ref[...], 0), axis=1, keepdims=True
            )
        )
    pid = jnp.concatenate(pids, axis=0) - c * 64
    pid2 = jnp.broadcast_to(pid, (2 * rows, 128)) - lane((2 * rows, 128)) // 64

    acc = jnp.zeros((2 * rows, 128), f32)
    for i in range(8):
        use(("s", i))
        scores = lax.dot_general(
            hid[...], sbuf[i], (((1,), (1,)), ((), ())), preferred_element_type=f32
        )
        for j in range(4):
            acc = acc + jnp.where(pid2 == 8 * i + 2 * j, scores[:, j * 128 : j * 128 + 128], 0.0)
        if i == SPLIT:
            forward(0)
    acc = acc + pltpu.roll(acc, 64, 1)
    low = lane((rows, 128)) < 64
    pack[...] = jnp.where(low, acc[:rows], acc[rows:])
    l_copies = []
    for step in range(1, 8):
        to = (tp + step) % 8
        source = pack.at[pl.ds(pl.multiple_of(to * 16, 16), 16)]
        l_copies.append(send(source, lrr.at[step - 1], l_sem, (step - 1,), c, to))

    own_piece(3)
    bs[...] = own[3, theirs, :]
    b_copy = send(bs, br, b_sem, (), 1 - c, tp)
    own_piece(2)
    forward(1)

    block = pl.ds(pl.multiple_of(tp * 16, 16), 16)
    total = pack[block, :]
    for step in range(1, 8):
        l_copies[step - 1].wait_recv()
        total = total + lrr[step - 1]
    lrs[...] = total.astype(bf16)
    lrg[block, :] = lrs[...]
    g_copies = []
    for step in range(1, 8):
        to = (tp + step) % 8
        g_copies.append(send(lrs, lrg.at[block], g_sem, (step - 1,), c, to))

    forward(2)

    for step in range(1, 8):
        g_copies[step - 1].wait_recv()
    packed = lrg[...].astype(f32)
    turned = pltpu.roll(packed, 64, 1)
    rank2 = jnp.concatenate(
        [jnp.where(low, packed, turned), jnp.where(low, turned, packed)], axis=0
    )
    for i in range(4):
        use(("e", i))
        weighted = jnp.concatenate(
            [jnp.where(pid2 == 16 * i + 2 * j, rank2, 0.0).astype(bf16) for j in range(8)],
            axis=1,
        )
        part = jnp.dot(weighted, ebuf[i], preferred_element_type=f32)
        if i == 0:
            delta[...] = part
        else:
            delta[...] += part
    ds_[...] = delta[theirs, :]
    d_copy = send(ds_, dr, d_sem, (), 1 - c, tp)

    own_cols = pl.ds(pl.multiple_of(c * half, half), half)
    other_cols = pl.ds(pl.multiple_of((1 - c) * half, half), half)
    b_copy.wait_recv()
    d_copy.wait_recv()
    base = [
        own[3, mine, :] + delta[mine, own_cols] + dr[:, own_cols],
        br[...] + delta[mine, other_cols] + dr[:, other_cols],
    ]
    for i, copies in ((1, z_copies), (2, z_copies), (0, x_copies)):
        for h in range(2):
            copies[3 if i == 0 else i, h].wait_recv()
            base[h] = base[h] + last[i, h].astype(f32)
    out_ref[:, own_cols] = base[0].astype(bf16)
    out_ref[:, other_cols] = base[1].astype(bf16)

    for copy in pending:
        copy.wait_send()


def local_fused(
    hidden,
    row_request_slots,
    requests,
    adapter_page_table,
    down_matrix,
    shrink_pool_pages,
    expand_pool_pages,
):
    rows, depth = hidden.shape
    pages, rank, width = expand_pool_pages.shape
    half = width // 2
    bf16, f32 = jnp.bfloat16, jnp.float32
    vmem = pl.BlockSpec(memory_space=pltpu.VMEM)
    hbm = pl.BlockSpec(memory_space=pl.ANY)
    V = pltpu.VMEM
    dma = pltpu.SemaphoreType.DMA
    flat = pages * rank
    return pl.pallas_call(
        fused_kernel,
        out_shape=jax.ShapeDtypeStruct((rows, width), bf16),
        in_specs=[vmem, vmem, vmem, hbm, hbm, hbm, hbm],
        out_specs=vmem,
        scratch_shapes=[
            V((2 * rows, depth), bf16),
            V((8, depth, half), bf16),
            V((8, flat // 8, depth), bf16),
            V((4, flat // 4, width), bf16),
            V((4, 2 * rows, half), f32),
            V((4, 2 * rows, half), bf16),
            V((3, 2 * rows, half), bf16),
            V((3, 2 * rows, half), bf16),
            V((2 * rows, half), bf16),
            V((3, 2, rows, half), bf16),
            V((rows, half), f32),
            V((rows, half), f32),
            V((2 * rows, width), f32),
            V((rows, width), f32),
            V((rows, width), f32),
            V((rows, 128), f32),
            V((7, 16, 128), f32),
            V((16, 128), bf16),
            V((rows, 128), bf16),
            dma((20,)),
            dma((3,)),
            dma((2, 8)),
            dma((2, 3, 2)),
            dma((2,)),
            dma((2,)),
            dma((2, 7)),
            dma((2, 7)),
        ],
        compiler_params=pltpu.CompilerParams(
            collective_id=0, has_side_effects=True, vmem_limit_bytes=60 * 1024 * 1024
        ),
    )(
        row_request_slots.reshape(-1, rows),
        requests,
        adapter_page_table.reshape(1, -1),
        hidden,
        down_matrix,
        shrink_pool_pages.reshape(flat, depth),
        expand_pool_pages.reshape(flat, width),
    )


def solution(mesh):
    return jax.shard_map(
        local_fused if mesh.shape["tp"] == 8 else local_general,
        mesh=mesh,
        in_specs=(
            P(("rep", "pool"), "tp"),
            P("rep"),
            P("rep", None),
            P(),
            P("tp", None),
            P("pool", None, "tp"),
            P("pool", None, "tp"),
        ),
        out_specs=P(("rep", "pool"), "tp"),
        check_vma=False,
    )
```

```python
import functools

import jax
import jax.numpy as jnp
from jax import lax
from jax.experimental import pallas as pl
from jax.experimental.pallas import tpu as pltpu
from jax.sharding import PartitionSpec as P

MESH = pl.DeviceIdType.MESH
DEPTH = 4
SPLIT = 3


def owner_split(adapters, adapter_page_table, per_holder_count):
    page_numbers = jnp.take(adapter_page_table, adapters, axis=0)
    return (page_numbers // per_holder_count, page_numbers % per_holder_count)


def shrink_select(rows_in, pages_a, onehot_picker):
    scores = jnp.einsum("rf,pkf->rpk", rows_in, pages_a, preferred_element_type=jnp.float32)
    return jnp.sum(scores * onehot_picker[:, :, None], axis=1)


def expand_choice_mask(rank_activation, expand_page_rows, onehot_picker):
    weighted = (onehot_picker[:, :, None] * rank_activation.astype(jnp.float32)[:, None, :]).astype(
        jnp.bfloat16
    )
    flat_rows = weighted.reshape(weighted.shape[0], -1)
    flat_pages = expand_page_rows.reshape(-1, expand_page_rows.shape[2])
    return jnp.dot(flat_rows, flat_pages, preferred_element_type=jnp.float32)


def local_general(
    hidden,
    row_request_slots,
    requests,
    adapter_page_table,
    down_matrix,
    shrink_pool_pages,
    expand_pool_pages,
):
    rows_dev = hidden.shape[0]
    per_holder_count = shrink_pool_pages.shape[0]
    pool_index = lax.axis_index("pool")
    partial_value = jnp.dot(hidden, down_matrix, preferred_element_type=jnp.float32)
    base_output = lax.psum_scatter(partial_value, "tp", scatter_dimension=1, tiled=True)
    owner_index, shard_local_pages = owner_split(requests, adapter_page_table, per_holder_count)
    holder_slots = (owner_index == pool_index)[:, :, None, None]
    empty_filler = jnp.zeros((), jnp.bfloat16)
    sent_shrink_pages = jnp.where(
        holder_slots, jnp.take(shrink_pool_pages, shard_local_pages, axis=0), empty_filler
    )
    sent_expand_pages = jnp.where(
        holder_slots, jnp.take(expand_pool_pages, shard_local_pages, axis=0), empty_filler
    )
    fetched_a, fetched_b = (
        lax.all_to_all(sent_shrink_pages, "pool", split_axis=0, concat_axis=0, tiled=True),
        lax.all_to_all(sent_expand_pages, "pool", split_axis=0, concat_axis=0, tiled=True),
    )
    pages_a = jnp.sum(fetched_a, axis=0)
    expand_page_rows = jnp.sum(fetched_b, axis=0)
    own_slots = lax.dynamic_slice_in_dim(row_request_slots, pool_index * rows_dev, rows_dev, 0)
    slot_range = jnp.arange(pages_a.shape[0], dtype=jnp.int32)
    onehot_picker = (own_slots[:, None] == slot_range[None, :]).astype(jnp.float32)
    shrink_part = shrink_select(hidden, pages_a, onehot_picker)
    rank_activation = lax.psum(shrink_part, "tp").astype(jnp.bfloat16)
    adapter_update = expand_choice_mask(rank_activation, expand_page_rows, onehot_picker)
    return (base_output + adapter_update).astype(jnp.bfloat16)


def fused_kernel(
    slots_ref,
    requests_ref,
    table_ref,
    hidden_ref,
    down_ref,
    shrink_ref,
    expand_ref,
    out_ref,
    hid,
    wbuf,
    sbuf,
    ebuf,
    own,
    xs,
    xr,
    zs,
    pair,
    last,
    bs,
    br,
    delta,
    ds_,
    dr,
    pack,
    lrr,
    lrs,
    lrg,
    load_sem,
    hid_sem,
    x_sem,
    z_sem,
    b_sem,
    d_sem,
    l_sem,
    g_sem,
):
    rep = lax.axis_index("rep")
    c = lax.axis_index("pool")
    tp = lax.axis_index("tp")
    z, x = tp // 2, tp % 2
    rows = hidden_ref.shape[0]
    half = out_ref.shape[1] // 2
    f32, bf16 = jnp.float32, jnp.bfloat16
    lane = lambda shape: lax.broadcasted_iota(jnp.int32, shape, 1)

    def dev(pool, t):
        return (rep, pool, t)

    near, far = z + 1 - 2 * (z % 2), (z + 2) % 4
    zdest = [3 - z, far, near, z]

    def column(zz, xx):
        return pl.multiple_of((zz * 2 + xx) * (2 * half) + c * half, half)

    loads = []
    keys = {}

    def add(key, source, target):
        k = len(loads)
        keys[key] = k
        loads.append(pltpu.make_async_copy(source, target, load_sem.at[k]))

    def add_down(key, slot, zz, xx):
        add(key, down_ref.at[:, pl.ds(column(zz, xx), half)], wbuf.at[slot])

    for i in range(4):
        add_down(("r", i), i, zdest[i], 1 - x)
    for i in (0, 1):
        add_down(("o", i), 4 + i, zdest[i], x)
    for i in range(8):
        add(("s", i), shrink_ref.at[pl.ds(i * 512, 512), :], sbuf.at[i])
    for i in (3, 2):
        add_down(("o", i), 4 + i, zdest[i], x)
    for i in range(4):
        add(("e", i), expand_ref.at[pl.ds(i * 1024, 1024), :], ebuf.at[i])

    mine = pl.ds(pl.multiple_of(c * rows, rows), rows)
    theirs = pl.ds(pl.multiple_of((1 - c) * rows, rows), rows)
    halves = (mine, theirs)
    hid_local = pltpu.make_async_copy(hidden_ref, hid.at[mine], hid_sem.at[2])
    hid_local.start()
    for k in range(DEPTH):
        loads[k].start()

    def use(key):
        k = keys[key]
        loads[k].wait()
        if k + DEPTH < len(loads):
            loads[k + DEPTH].start()

    barrier = pltpu.get_barrier_semaphore()
    for step in range(1, 8):
        pl.semaphore_signal(barrier, inc=1, device_id=dev(c, (tp + step) % 8), device_id_type=MESH)
    xn = z * 2 + 1 - x
    for t in (tp, xn, near * 2 + x, far * 2 + x):
        pl.semaphore_signal(barrier, inc=1, device_id=dev(1 - c, t), device_id_type=MESH)
    pl.semaphore_wait(barrier, 11)

    pending = []

    def send(src, dst, sems, index, pool, t):
        copy = pltpu.make_async_remote_copy(
            src_ref=src, dst_ref=dst,
            send_sem=sems.at[(0, *index)], recv_sem=sems.at[(1, *index)],
            device_id=dev(pool, t), device_id_type=MESH,
        )
        copy.start()
        pending.append(copy)
        return copy

    hid_swap = pltpu.make_async_remote_copy(
        src_ref=hidden_ref, dst_ref=hid.at[mine],
        send_sem=hid_sem.at[0], recv_sem=hid_sem.at[1],
        device_id=dev(1 - c, tp), device_id_type=MESH,
    )
    hid_swap.start()
    x_copies = {}

    def send_x(i, h):
        if i < 3:
            pool, target = c, xr.at[i, halves[h]]
        else:
            pool, target = (c, 1 - c)[h], last.at[0, h]
        x_copies[i, h] = send(xs.at[i, halves[h]], target, x_sem, (2 * i + h,), pool, xn)

    hid_local.wait()
    use(("r", 0))
    for h in range(2):
        if h == 1:
            hid_swap.wait()
        xs[0, halves[h]] = jnp.dot(
            hid[halves[h], :], wbuf[0], preferred_element_type=f32
        ).astype(bf16)
        send_x(0, h)
    for i in range(1, 4):
        use(("r", i))
        xs[i] = jnp.dot(hid[...], wbuf[i], preferred_element_type=f32).astype(bf16)
        if i == 1:
            for h in range(2):
                send_x(i, h)

    def own_piece(i):
        use(("o", i))
        own[i] = jnp.dot(hid[...], wbuf[4 + i], preferred_element_type=f32)

    z_copies = {}

    def forward(i):
        for h in range(2):
            part = halves[h]
            x_copies[i, h].wait_recv()
            total = own[i, part] + xr[i, part].astype(f32)
            if i == 1:
                z_copies[0, h].wait_recv()
                total = total + pair[part, :].astype(f32)
            zs[i, part] = total.astype(bf16)
            if i == 0:
                pool, target = c, pair.at[part]
            else:
                pool, target = (c, 1 - c)[h], last.at[i, h]
            z_copies[i, h] = send(
                zs.at[i, part], target, z_sem, (i, h), pool, (far if i == 1 else near) * 2 + x
            )

    own_piece(0)
    own_piece(1)

    pids = []
    for s in range(2):
        slot = jnp.transpose(jnp.broadcast_to(slots_ref[s : s + 1, :], (rows, rows)))
        adapter = jnp.sum(
            jnp.where(lane((rows, 32)) == slot[:, :32], requests_ref[s : s + 1, :], 0),
            axis=1, keepdims=True,
        )
        pids.append(
            jnp.sum(
                jnp.where(lane((rows, 128)) == adapter, table_ref[...], 0), axis=1, keepdims=True
            )
        )
    pid = jnp.concatenate(pids, axis=0) - c * 64
    pid2 = jnp.broadcast_to(pid, (2 * rows, 128)) - lane((2 * rows, 128)) // 64

    acc = jnp.zeros((2 * rows, 128), f32)
    for i in range(8):
        use(("s", i))
        scores = lax.dot_general(
            hid[...], sbuf[i], (((1,), (1,)), ((), ())), preferred_element_type=f32
        )
        for j in range(4):
            acc = acc + jnp.where(pid2 == 8 * i + 2 * j, scores[:, j * 128 : j * 128 + 128], 0.0)
        if i == SPLIT:
            forward(0)
    acc = acc + pltpu.roll(acc, 64, 1)
    low = lane((rows, 128)) < 64
    pack[...] = jnp.where(low, acc[:rows], acc[rows:])
    l_copies = []
    for step in range(1, 8):
        to = (tp + step) % 8
        source = pack.at[pl.ds(pl.multiple_of(to * 16, 16), 16)]
        l_copies.append(send(source, lrr.at[step - 1], l_sem, (step - 1,), c, to))

    for h in range(2):
        send_x(2, h)
    own_piece(3)
    bs[...] = own[3, theirs, :]
    b_copy = send(bs, br, b_sem, (), 1 - c, tp)
    own_piece(2)

    block = pl.ds(pl.multiple_of(tp * 16, 16), 16)
    total = pack[block, :]
    for step in range(1, 8):
        l_copies[step - 1].wait_recv()
        total = total + lrr[step - 1]
    lrs[...] = total.astype(bf16)
    lrg[block, :] = lrs[...]
    g_copies = []
    for step in range(1, 8):
        to = (tp + step) % 8
        g_copies.append(send(lrs, lrg.at[block], g_sem, (step - 1,), c, to))

    for h in range(2):
        send_x(3, h)
    forward(1)
    forward(2)

    for step in range(1, 8):
        g_copies[step - 1].wait_recv()
    packed = lrg[...].astype(f32)
    turned = pltpu.roll(packed, 64, 1)
    rank2 = jnp.concatenate(
        [jnp.where(low, packed, turned), jnp.where(low, turned, packed)], axis=0
    )
    for i in range(4):
        use(("e", i))
        weighted = jnp.concatenate(
            [jnp.where(pid2 == 16 * i + 2 * j, rank2, 0.0).astype(bf16) for j in range(8)],
            axis=1,
        )
        part = jnp.dot(weighted, ebuf[i], preferred_element_type=f32)
        if i == 0:
            delta[...] = part
        else:
            delta[...] += part
    ds_[...] = delta[theirs, :]
    d_copy = send(ds_, dr, d_sem, (), 1 - c, tp)

    own_cols = pl.ds(pl.multiple_of(c * half, half), half)
    other_cols = pl.ds(pl.multiple_of((1 - c) * half, half), half)
    b_copy.wait_recv()
    d_copy.wait_recv()
    base = [
        own[3, mine, :] + delta[mine, own_cols] + dr[:, own_cols],
        br[...] + delta[mine, other_cols] + dr[:, other_cols],
    ]
    for i, copies in ((1, z_copies), (2, z_copies), (0, x_copies)):
        for h in range(2):
            copies[3 if i == 0 else i, h].wait_recv()
            base[h] = base[h] + last[i, h].astype(f32)
    out_ref[:, own_cols] = base[0].astype(bf16)
    out_ref[:, other_cols] = base[1].astype(bf16)

    for copy in pending:
        copy.wait_send()


def local_fused(
    hidden,
    row_request_slots,
    requests,
    adapter_page_table,
    down_matrix,
    shrink_pool_pages,
    expand_pool_pages,
):
    rows, depth = hidden.shape
    pages, rank, width = expand_pool_pages.shape
    half = width // 2
    bf16, f32 = jnp.bfloat16, jnp.float32
    vmem = pl.BlockSpec(memory_space=pltpu.VMEM)
    hbm = pl.BlockSpec(memory_space=pl.ANY)
    V = pltpu.VMEM
    dma = pltpu.SemaphoreType.DMA
    flat = pages * rank
    return pl.pallas_call(
        fused_kernel,
        out_shape=jax.ShapeDtypeStruct((rows, width), bf16),
        in_specs=[vmem, vmem, vmem, hbm, hbm, hbm, hbm],
        out_specs=vmem,
        scratch_shapes=[
            V((2 * rows, depth), bf16),
            V((8, depth, half), bf16),
            V((8, flat // 8, depth), bf16),
            V((4, flat // 4, width), bf16),
            V((4, 2 * rows, half), f32),
            V((4, 2 * rows, half), bf16),
            V((3, 2 * rows, half), bf16),
            V((3, 2 * rows, half), bf16),
            V((2 * rows, half), bf16),
            V((3, 2, rows, half), bf16),
            V((rows, half), f32),
            V((rows, half), f32),
            V((2 * rows, width), f32),
            V((rows, width), f32),
            V((rows, width), f32),
            V((rows, 128), f32),
            V((7, 16, 128), f32),
            V((16, 128), bf16),
            V((rows, 128), bf16),
            dma((20,)),
            dma((3,)),
            dma((2, 8)),
            dma((2, 3, 2)),
            dma((2,)),
            dma((2,)),
            dma((2, 7)),
            dma((2, 7)),
        ],
        compiler_params=pltpu.CompilerParams(
            collective_id=0, has_side_effects=True, vmem_limit_bytes=60 * 1024 * 1024
        ),
    )(
        row_request_slots.reshape(-1, rows),
        requests,
        adapter_page_table.reshape(1, -1),
        hidden,
        down_matrix,
        shrink_pool_pages.reshape(flat, depth),
        expand_pool_pages.reshape(flat, width),
    )


def solution(mesh):
    return jax.shard_map(
        local_fused if mesh.shape["tp"] == 8 else local_general,
        mesh=mesh,
        in_specs=(
            P(("rep", "pool"), "tp"),
            P("rep"),
            P("rep", None),
            P(),
            P("tp", None),
            P("pool", None, "tp"),
            P("pool", None, "tp"),
        ),
        out_specs=P(("rep", "pool"), "tp"),
        check_vma=False,
    )
```
